512 devices in a mesh: dom: 64 (over y, z), row: 8 (over x, core).
Axes of the slice: x: 4, y: 4, z: 16, core: 2. Of those that a mesh axis runs over, the one named last changes fastest.
Arguments:
- embedding: float32 [32768, 400], P(('dom', 'row')), may hold values from -1.5 to 1.5
- adagrad: float32 [32768], P(('dom', 'row')), may hold values from 0.05 to 1
- relation: bfloat16 [4096, 400], replicated, may hold values from -4.1875 to 4.1875
- offsets: int32 [2], replicated, may hold values from 1 to 63
- counts: int32 [2, 512], P(None, ('dom', 'row')), may hold values from 1 to 2048, 524288 in all within a row
- lhs_index: int32 [2, 1048576], P(None, ('dom', 'row')), may hold values from 0 to 511
- rhs_index: int32 [2, 1048576], P(None, ('dom', 'row')), may hold values from 0 to 511
- rel_ids: int32 [2, 1048576], P(None, ('dom', 'row')), may hold values from 0 to 4095
- neg_index: int32 [2, 64, 128], P(None, 'dom'), may hold values from 0 to 511
Outputs:
- embedding_out: float32 [32768, 400], P(('dom', 'row'))
- adagrad_out: float32 [32768], P(('dom', 'row'))
The draws below stay inside these ranges and needn't reach their ends.
Inputs may be any that keep to these rules, and one draw needn't show every extreme that they name: In every round some device has all 2048 slots live; the counts of one round add up to 524288.
All inputs are finite; a program needn't handle non-finite values.
Results may differ from the reference program's by a relative error of at most 0.0018.
Values may be sent and summed in bfloat16 or wider, within the bound.
A program may use at most 64 MiB of HBM per device.

```python
import math
import jax
import jax.numpy as jnp
import numpy as np
from jax import lax

D = 400
NREL = 4096
NEG = 128
ROUNDS = 2
R_DEV = 64
E_DEV = 2048
ROWS = 512
ENTITIES = 32768
N_DOM = 64
N_ROW = 8
DEVICES = 512


def place_ends(array, key, smallest, largest):
    spot = [jax.random.randint(jax.random.fold_in(key, axis), (), 0, length) for axis, length in enumerate(array.shape)]
    longest = array.shape.index(max(array.shape))
    neighbour = spot[:longest] + [(spot[longest] + 1) % array.shape[longest]] + spot[longest + 1:]
    return array.at[tuple(spot)].set(smallest).at[tuple(neighbour)].set(largest)


def level_of(stream_key, dims, shards, least, largest):
    factor_of = 1.0
    for dim, parts in shards:
        draws = jax.random.uniform(jax.random.fold_in(jax.random.fold_in(stream_key, 6), dim), (parts,), jnp.float32, least / len(shards), largest / len(shards))
        factor_of = factor_of * jnp.repeat(jnp.exp(draws), dims[dim] // parts).reshape((-1,) + (1,) * (len(dims) - 1 - dim))
    return factor_of


def cumulative_ranks(amount, skew):
    weights = [(1 << 20) // math.isqrt(rank ** skew) + 1 for rank in range(1, amount + 1)]
    deviation = 1 + sum(weights) // (1 << 30)
    return np.cumsum(np.array([max(1, weight // deviation) for weight in weights]))


def skewed_ids(own_key, shape, amount, lean):
    grid = cumulative_ranks(amount, lean)
    ticket = jax.random.randint(jax.random.fold_in(own_key, 1), shape, 0, int(grid[amount - 1]))
    standing = jnp.searchsorted(jnp.asarray(grid, jnp.int32), ticket, side="right")
    return jax.random.permutation(jax.random.fold_in(own_key, 2), amount)[standing].astype(jnp.int32)


def length_profile(count, total, reach, slope):
    loads = [(1 << 20) // math.isqrt(rank ** slope) + 1 for rank in range(2, count + 1)]
    rest, given = total - reach - (count - 1), [1] * (count - 1)
    while rest > 0:
        candidates = [i for i in range(count - 1) if given[i] < reach]
        whole, budget = sum([loads[i] for i in candidates]), rest
        for i in candidates:
            addition = min(reach - given[i], max(1, budget * loads[i] // whole), rest)
            given[i] = given[i] + addition
            rest = rest - addition
    return np.array([reach] + given)


def ragged(own_key, number_of, total, bound, lean):
    if number_of == 2:
        one = jax.random.randint(own_key, (), max(1, total - bound), min(bound, total - 1) + 1)
        return jnp.stack([one, total - one])
    lengths = jnp.asarray(length_profile(number_of, total, bound, lean), jnp.int32)
    pairs = (number_of - 1) // 2
    giver, sink = lengths[1:1 + 2 * pairs:2], lengths[2:2 + 2 * pairs:2]
    room = jnp.minimum(giver - 1, bound - sink)
    passed = jax.random.randint(jax.random.fold_in(own_key, 1), (pairs,), 0, 1 << 20) % (room + 1)
    lengths = lengths.at[1:1 + 2 * pairs:2].set(giver - passed).at[2:2 + 2 * pairs:2].set(sink + passed)
    return lengths[jax.random.permutation(jax.random.fold_in(own_key, 2), number_of)]


def bell_draw(key, shape, deviation, bound, split=(), held_as=jnp.bfloat16):
    entries = deviation * jax.random.normal(key, shape, jnp.float32)
    if split:
        entries = entries * level_of(key, shape, split, -0.22, 0.18)
    return jnp.clip(entries, -bound, bound).astype(held_as)


def setup_inputs(seed: int = 0) -> dict:
    arg_keys = jax.random.split(jax.random.key(seed), 10)
    return {
        "embedding": bell_draw(arg_keys[0], (ENTITIES, D), 0.25, 1.5, ((0, 512),), jnp.float32),
        "adagrad": jnp.clip(jnp.exp(math.log(1.0) - 2.9957323 * jax.random.uniform(arg_keys[1], (ENTITIES,), jnp.float32) ** level_of(arg_keys[1], (ENTITIES,), ((0, 512),), -0.2, 0.2)), 0.05, 1.0),
        "relation": bell_draw(arg_keys[2], (NREL, D), 0.7, 4.1875),
        "offsets": jax.random.randint(arg_keys[3], (ROUNDS,), 1, N_DOM).astype(jnp.int32),
        "counts": jax.vmap(lambda own: ragged(own, DEVICES, DEVICES * E_DEV // 2, E_DEV, 2))(jax.random.split(arg_keys[4], ROUNDS)).reshape((ROUNDS, DEVICES)).astype(jnp.int32),
        "lhs_index": place_ends(jax.random.randint(arg_keys[5], (ROUNDS, DEVICES * E_DEV), 0, ROWS), jax.random.fold_in(arg_keys[5], 1), 0, ROWS - 1).astype(jnp.int32),
        "rhs_index": place_ends(jax.random.randint(arg_keys[6], (ROUNDS, DEVICES * E_DEV), 0, ROWS), jax.random.fold_in(arg_keys[6], 1), 0, ROWS - 1).astype(jnp.int32),
        "rel_ids": place_ends(skewed_ids(arg_keys[7], (ROUNDS, DEVICES * E_DEV), NREL, 2), jax.random.fold_in(arg_keys[7], 3), 0, NREL - 1).astype(jnp.int32),
        "neg_index": place_ends(jax.random.randint(arg_keys[8], (ROUNDS, N_DOM, NEG), 0, ROWS), jax.random.fold_in(arg_keys[8], 1), 0, ROWS - 1).astype(jnp.int32),
    }


learn_rate = 0.1
edge_block = 512

def complex_times(heads, rel_rows):
    half_width = heads.shape[1] // 2
    head_re, head_im = (heads[:, :half_width], heads[:, half_width:])
    rel_re, rel_im = (rel_rows[:, :half_width], rel_rows[:, half_width:])
    return jnp.concatenate([head_re * rel_re - head_im * rel_im, head_re * rel_im + head_im * rel_re], axis=1)

def complex_back(grads, rel_rows):
    half_width = grads.shape[1] // 2
    grad_re, grad_im = (grads[:, :half_width], grads[:, half_width:])
    rel_re, rel_im = (rel_rows[:, :half_width], rel_rows[:, half_width:])
    return jnp.concatenate([grad_re * rel_re + grad_im * rel_im, grad_im * rel_re - grad_re * rel_im], axis=1)

def block_grads(head_panel, tail_panel, neg_rows, relation, head_ids, tail_ids, rel_list, is_live):
    heads = head_panel[head_ids].astype(jnp.float32)
    tails = tail_panel[tail_ids].astype(jnp.float32)
    rel_rows = relation[rel_list].astype(jnp.float32)
    query = complex_times(heads, rel_rows).astype(jnp.bfloat16)
    query_f = query.astype(jnp.float32)
    positive = lax.optimization_barrier(jnp.sum(query_f * tails, axis=1))
    negative = lax.dot_general(query, neg_rows, (((1,), (1,)), ((), ())), preferred_element_type=jnp.float32)
    pos_weight = jnp.where(is_live, -jax.nn.sigmoid(-positive), 0.0)
    neg_weight = jnp.where(is_live[:, None], jax.nn.sigmoid(negative) / neg_rows.shape[0], 0.0).astype(jnp.bfloat16)
    query_grad = pos_weight[:, None] * tails + jnp.dot(neg_weight, neg_rows, preferred_element_type=jnp.float32)
    head_grad = complex_back(query_grad, rel_rows)
    tail_grad = pos_weight[:, None] * query_f
    neg_grad = lax.dot_general(neg_weight, query, (((0,), (0,)), ((), ())), preferred_element_type=jnp.float32)
    return (head_grad, tail_grad, neg_grad)

def group_grads(head_panel, tail_panel, neg_ids, relation, head_ids, tail_ids, rel_list, count_list):
    slot_total = head_ids.shape[0]
    per_device = slot_total // count_list.shape[0]
    block_len = min(edge_block, per_device)
    slot_ids = jnp.arange(slot_total, dtype=jnp.int32)
    live_all = slot_ids % per_device < count_list[slot_ids // per_device]
    neg_rows = tail_panel[neg_ids]
    row_total = head_panel.shape[0]
    col_total = head_panel.shape[1]

    def cut_block(values, first):
        return lax.dynamic_slice_in_dim(values, first, block_len)

    def step(accums, block_no):
        head_acc, tail_acc, neg_acc = accums
        first = block_no * block_len
        head_part = cut_block(head_ids, first)
        tail_part = cut_block(tail_ids, first)
        head_grad, tail_grad, neg_grad = block_grads(head_panel, tail_panel, neg_rows, relation, head_part, tail_part, cut_block(rel_list, first), cut_block(live_all, first))
        return ((head_acc.at[head_part].add(head_grad), tail_acc.at[tail_part].add(tail_grad), neg_acc + neg_grad), None)
    zero_rows = jnp.zeros((row_total, col_total), jnp.float32)
    zero_negs = jnp.zeros((neg_ids.shape[0], col_total), jnp.float32)
    (head_acc, tail_acc, neg_acc), _ = lax.scan(step, (zero_rows, zero_rows, zero_negs), jnp.arange(slot_total // block_len, dtype=jnp.int32))
    return (head_acc, tail_acc.at[neg_ids].add(neg_acc))

def reference(embedding, adagrad, relation, offsets, counts, lhs_index, rhs_index, rel_ids, neg_index):
    row_total = R_DEV * N_ROW
    groups = jnp.arange(N_DOM, dtype=jnp.int32)
    current = embedding
    squares_sum = adagrad
    for round_index in range(ROUNDS):
        working = current.astype(jnp.bfloat16).reshape(N_DOM, row_total, D)
        offset_now = offsets[round_index]
        heads_all = lhs_index[round_index].reshape(N_DOM, N_ROW * E_DEV)
        tails_all = rhs_index[round_index].reshape(N_DOM, N_ROW * E_DEV)
        rels_all = rel_ids[round_index].reshape(N_DOM, N_ROW * E_DEV)
        counts_all = counts[round_index].reshape(N_DOM, N_ROW)
        negs_all = neg_index[round_index]

        def one_group(worker):
            partner = (worker + offset_now) % N_DOM
            return group_grads(working[worker], working[partner], negs_all[worker], relation, heads_all[worker], tails_all[worker], rels_all[worker], counts_all[worker])
        head_sums, tail_sums = lax.map(one_group, groups)
        gradient = head_sums + tail_sums[(groups - offset_now) % N_DOM]
        gradient = gradient.reshape(N_DOM * row_total, D)
        squares_sum = squares_sum + lax.optimization_barrier(jnp.mean(gradient * gradient, axis=1))
        current = current - learn_rate * gradient / jnp.sqrt(squares_sum)[:, None]
    return (current, squares_sum)
```

```python
import jax
import jax.numpy as jnp
from jax import lax
from jax.experimental import pallas as pl
from jax.experimental.pallas import tpu as pltpu
from jax.sharding import PartitionSpec as P

ROUNDS = 2
D = 400
HALF = 200
WIDE = 512
PART = 4
LANES = 128
SUM_PIECE, SUM_LANE = 1, 127
ND, NR, NX = 64, 8, 4
R_DEV = 64
ROWS = 512
EDGES = 2048
NREL = 4096
NEG = 128
BLOCK = 256
BLOCKS = EDGES // BLOCK
LEARN = 0.1
MESH = pl.DeviceIdType.MESH
F32, BF16 = jnp.float32, jnp.bfloat16
NT = (((1,), (1,)), ((), ()))
TN = (((0,), (0,)), ((), ()))


def dot(a, b):
    return jnp.dot(a, b, preferred_element_type=F32)


def remote(src, dst, send, recv, device):
    return pltpu.make_async_remote_copy(
        src_ref=src, dst_ref=dst, send_sem=send, recv_sem=recv, device_id=device, device_id_type=MESH
    )


def panel_order(ids):
    owner = ids // R_DEV
    return (owner % 2) * (ROWS // 2) + (owner // 2) * R_DEV + ids % R_DEV


def as_column(row):
    return jnp.transpose(jnp.broadcast_to(row, (LANES, row.shape[1])))


def one_hot_rows(row, count):
    column = as_column(row)
    lane = lax.broadcasted_iota(jnp.int32, column.shape, 1)
    pieces = [(column == lane + first).astype(F32).astype(BF16) for first in range(0, count, LANES)]
    return jnp.concatenate(pieces, axis=1)


def one_hot_columns(row, count):
    place = lax.broadcasted_iota(jnp.int32, (count, row.shape[1]), 0)
    return (row == place).astype(F32).astype(BF16)


def split(value):
    high = value.astype(BF16)
    return high, (value - high.astype(F32)).astype(BF16)


def kernel(
    offsets, counts, state0, head0, lhs, rhs, rel, neg, relation,
    out,
    raw, table, rel_rows, hot_h, hot_t, hot_ht, hot_tt, query, grad_h, grad_t, neg_sum, neg_rows,
    state, work, stage, tail_in, head_in, shard_h, shard_t, panel_h, panel_t,
    acc_h, acc_t, near_h, near_t, far_send, far_h, far_t, row_send, got_h, got_t,
    raw_sem, a2a_send, a2a_recv, ag_send, ag_recv, rs_send, rs_recv,
):
    me, row = lax.axis_index("dom"), lax.axis_index("row")
    x, core = row // 2, lax.rem(row, 2)
    sibling = x * 2 + 1 - core
    slot = core * NX + x

    barrier = pltpu.get_barrier_semaphore()

    def greet(j, c):
        pl.semaphore_signal(barrier, inc=1, device_id=(lax.rem(me + j, ND), row), device_id_type=MESH)
        return c

    lax.fori_loop(1, ND, greet, 0)
    for j in range(1, NR):
        pl.semaphore_signal(barrier, inc=1, device_id=(me, lax.rem(row + j, NR)), device_id_type=MESH)

    def relation_block(k, b):
        at = pl.ds(pl.multiple_of(b * BLOCK, BLOCK), BLOCK)
        hot = one_hot_rows(rel[pl.ds(k, 1), at], NREL)
        rel_rows[k, at, :] = dot(hot, table[...]).astype(BF16)

    def relation_blocks(k, first, last):
        def step(b, c):
            relation_block(k, b)
            return c

        lax.fori_loop(first, last, step, 0)

    def selectors(k):
        def step(b, c):
            at = pl.ds(pl.multiple_of(b * BLOCK, BLOCK), BLOCK)
            head_ids = panel_order(lhs[pl.ds(k, 1), at])
            tail_ids = panel_order(rhs[pl.ds(k, 1), at])
            hot_h[at, :] = one_hot_rows(head_ids, ROWS)
            hot_t[at, :] = one_hot_rows(tail_ids, ROWS)
            hot_ht[:, at] = one_hot_columns(head_ids, ROWS)
            hot_tt[:, at] = one_hot_columns(tail_ids, ROWS)
            return c

        lax.fori_loop(0, BLOCKS, step, 0)

    def queries(k):
        panel = panel_h[k].reshape(ROWS, WIDE)

        def step(b, c):
            at = pl.ds(pl.multiple_of(b * BLOCK, BLOCK), BLOCK)
            heads = dot(hot_h[at, :], panel)
            rels = rel_rows[k, at, :].astype(F32)
            h_re, h_im = heads[:, :256], heads[:, 256:]
            c_re, c_im = rels[:, :256], rels[:, 256:]
            query[at, :256] = (h_re * c_re - h_im * c_im).astype(BF16)
            query[at, 256:] = (h_re * c_im + h_im * c_re).astype(BF16)
            return c

        lax.fori_loop(0, BLOCKS, step, 0)

    def edge_grads(k):
        panel = panel_t[k].reshape(ROWS, WIDE)
        neg_ids = panel_order(neg[pl.ds(k, 1), :])
        neg_rows[...] = dot(one_hot_rows(neg_ids, ROWS), panel).astype(BF16)
        neg_sum[...] = jnp.zeros_like(neg_sum)
        count = counts[k, 0]

        def step(b, c):
            at = pl.ds(pl.multiple_of(b * BLOCK, BLOCK), BLOCK)
            tails = dot(hot_t[at, :], panel)
            q = query[at, :]
            q_f = q.astype(F32)
            positive = jnp.sum(q_f * tails, axis=1, keepdims=True)
            negative = lax.dot_general(q, neg_rows[...], NT, preferred_element_type=F32)
            live = b * BLOCK + lax.broadcasted_iota(jnp.int32, (BLOCK, 1), 0) < count
            pos_weight = jnp.where(live, -1.0 / (1.0 + jnp.exp(positive)), 0.0)
            neg_weight = jnp.where(live, (1.0 / NEG) / (1.0 + jnp.exp(-negative)), 0.0).astype(BF16)
            g = pos_weight * tails + dot(neg_weight, neg_rows[...])
            rels = rel_rows[k, at, :].astype(F32)
            g_re, g_im = g[:, :256], g[:, 256:]
            c_re, c_im = rels[:, :256], rels[:, 256:]
            high, low = split(g_re * c_re + g_im * c_im)
            grad_h[0, at, :256] = high
            grad_h[1, at, :256] = low
            high, low = split(g_im * c_re - g_re * c_im)
            grad_h[0, at, 256:] = high
            grad_h[1, at, 256:] = low
            high, low = split(pos_weight * q_f)
            grad_t[0, at, :] = high
            grad_t[1, at, :] = low
            neg_sum[...] += lax.dot_general(neg_weight, q, TN, preferred_element_type=F32)
            return c

        lax.fori_loop(0, BLOCKS, step, 0)

    def tail_sums(k):
        hot_n = one_hot_columns(panel_order(neg[pl.ds(k, 1), :]), ROWS)
        high, low = split(neg_sum[...])
        total = dot(hot_tt[...], grad_t[0]) + dot(hot_tt[...], grad_t[1]) + dot(hot_n, high) + dot(hot_n, low)
        acc_t[k] = total.reshape(acc_t.shape[1:])

    def head_sums(k):
        total = dot(hot_ht[...], grad_h[0]) + dot(hot_ht[...], grad_h[1])
        acc_h[k] = total.reshape(acc_h.shape[1:])

    def spread(number, src, dst):
        def step(j, c):
            t = lax.rem(me + j, ND)
            remote(src.at[t], dst.at[me], a2a_send.at[number], a2a_recv.at[number], (t, row)).start()
            return c

        lax.fori_loop(1, ND, step, 0)
        dst[me] = src[me]

    def spread_wait(number, src, dst):
        most = pl.ds(0, ND - 1)
        remote(src.at[most], dst.at[most], a2a_send.at[number], a2a_recv.at[number], (lax.rem(me + 1, ND), row)).wait()

    def rotated(k, src, dst, forward):
        by = offsets[k]
        shift = by if forward else ND - by

        def step(j, c):
            dst[j] = src[lax.rem(j + shift, ND)]
            return c

        lax.fori_loop(0, ND, step, 0)

    def gather_copies(number, src, panel):
        out_copies = []
        for j in (2, 1, 3):
            t = lax.rem(x + j, NX) * 2 + core
            out_copies.append(
                remote(src, panel.at[slot], ag_send.at[number, j], ag_recv.at[number, j], (me, t))
            )
        own = remote(src, panel.at[slot], ag_send.at[number, 0], ag_recv.at[number, 0], (me, sibling))
        return out_copies, own

    def gather_start(number, src, panel):
        out_copies, own = gather_copies(number, src, panel)
        for copy in out_copies:
            copy.start()
        own.start()
        panel[slot] = src[...]

    def gather_finish(number, src, panel):
        out_copies, own = gather_copies(number, src, panel)
        passed = []
        for j, copy in ((1, out_copies[1]), (3, out_copies[2]), (2, out_copies[0])):
            copy.wait_recv()
            place = core * NX + lax.rem(x + NX - j, NX)
            onward = remote(
                panel.at[place], panel.at[place], ag_send.at[number, NX + j], ag_recv.at[number, NX + j], (me, sibling)
            )
            onward.start()
            passed.append(onward)
        for copy in out_copies:
            copy.wait_send()
        own.wait()
        for copy in passed:
            copy.wait()

    def near_copy(number, acc, near):
        other = pl.ds((1 - core) * NX, NX)
        return remote(acc.at[other], near, rs_send.at[number, 0], rs_recv.at[number, 0], (me, sibling))

    def far_copies(number, far):
        copies = []
        for j in (2, 1, 3):
            t = lax.rem(x + j, NX)
            copies.append(
                remote(
                    far_send.at[number, t], far.at[j], rs_send.at[number, j], rs_recv.at[number, j], (me, t * 2 + core)
                )
            )
        return copies

    def sum_near(number, acc, near, far):
        near_copy(number, acc, near).wait()
        near[...] = near[...] + acc[pl.ds(core * NX, NX)]
        far_send[number] = near[...].astype(BF16)
        for copy in far_copies(number, far):
            copy.start()

    def sum_far(number, near, far):
        for copy in far_copies(number, far):
            copy.wait()
        return near[x] + (far[1].astype(F32) + far[2].astype(F32) + far[3].astype(F32))

    def is_sum():
        piece = lax.broadcasted_iota(jnp.int32, state.shape, 1)
        lane = lax.broadcasted_iota(jnp.int32, state.shape, 2)
        return (piece == SUM_PIECE) & (lane == SUM_LANE)

    def to_work():
        work[...] = jnp.where(is_sum(), 0.0, state[...]).astype(BF16)

    def update(k):
        rotated(k, got_t.at[k], stage.at[2 + k], False)
        gradient = got_h[k].astype(F32) + stage[2 + k].astype(F32)
        at_sum = is_sum()
        now = state[...]
        squares = jnp.sum(jnp.where(at_sum, now, 0.0), axis=(1, 2), keepdims=True)
        squares = squares + jnp.sum(gradient * gradient, axis=(1, 2), keepdims=True) / D
        state[...] = jnp.where(at_sum, squares, now - LEARN * gradient / jnp.sqrt(squares))

    def to_rows(value):
        return value.reshape(R_DEV, PART, LANES).astype(BF16)

    def to_shard(value):
        return value.astype(F32).reshape(R_DEV, WIDE).astype(BF16)

    fetch = pltpu.make_async_copy(relation, raw, raw_sem.at[0])
    fetch.start()
    selectors(0)
    fetch.wait()
    from_col = lax.broadcasted_iota(jnp.int32, (D, WIDE), 0)
    to_col = lax.broadcasted_iota(jnp.int32, (D, WIDE), 1)
    widen = (to_col == jnp.where(from_col < HALF, from_col, from_col + 56)).astype(F32).astype(BF16)

    def widen_step(b, c):
        at = pl.ds(pl.multiple_of(b * BLOCK, BLOCK), BLOCK)
        table[at, :] = dot(raw[at, :], widen).astype(BF16)
        return c

    lax.fori_loop(0, NREL // BLOCK, widen_step, 0)
    relation_blocks(0, 0, 2)

    pl.semaphore_wait(barrier, ND - 1 + NR - 1)
    spread(0, state0, state)
    gather_start(0, head0, panel_h.at[0])
    relation_blocks(0, 2, 6)
    gather_finish(0, head0, panel_h.at[0])
    spread_wait(0, state0, state)
    to_work()
    rotated(0, work, stage.at[0], True)
    spread(1, stage.at[0], tail_in.at[0])
    relation_blocks(0, 6, 8)
    queries(0)
    spread_wait(1, stage.at[0], tail_in.at[0])
    shard_t[0] = to_shard(tail_in[0])
    gather_start(1, shard_t.at[0], panel_t.at[0])
    relation_blocks(1, 0, 3)
    gather_finish(1, shard_t.at[0], panel_t.at[0])

    for k in range(ROUNDS):
        if k > 0:
            spread_wait(4, work, head_in)
            shard_h[...] = to_shard(head_in[...])
            gather_start(2, shard_h, panel_h.at[1])
            spread_wait(5, stage.at[1], tail_in.at[1])
            shard_t[1] = to_shard(tail_in[1])
            gather_start(3, shard_t.at[1], panel_t.at[1])
            gather_finish(2, shard_h, panel_h.at[1])
            queries(1)
            gather_finish(3, shard_t.at[1], panel_t.at[1])
        edge_grads(k)
        tail_sums(k)
        near_copy(2 * k, acc_t.at[k], near_t.at[k]).start()
        head_sums(k)
        near_copy(2 * k + 1, acc_h.at[k], near_h.at[k]).start()
        sum_near(2 * k, acc_t.at[k], near_t.at[k], far_t.at[k])
        sum_near(2 * k + 1, acc_h.at[k], near_h.at[k], far_h.at[k])
        if k == 0:
            relation_blocks(1, 3, 6)
        row_send[2 * k] = to_rows(sum_far(2 * k, near_t.at[k], far_t.at[k]))
        spread(2 + 4 * k, row_send.at[2 * k], got_t.at[k])
        row_send[2 * k + 1] = to_rows(sum_far(2 * k + 1, near_h.at[k], far_h.at[k]))
        spread(3 + 4 * k, row_send.at[2 * k + 1], got_h.at[k])
        if k == 0:
            relation_blocks(1, 6, 8)
            selectors(1)
        spread_wait(2 + 4 * k, row_send.at[2 * k], got_t.at[k])
        spread_wait(3 + 4 * k, row_send.at[2 * k + 1], got_h.at[k])
        update(k)
        if k == 0:
            to_work()
            spread(4, work, head_in)
            rotated(1, work, stage.at[1], True)
            spread(5, stage.at[1], tail_in.at[1])
    spread(8, state, out)
    spread_wait(8, state, out)


def body(embedding, adagrad, relation, offsets, counts, lhs_index, rhs_index, rel_ids, neg_index):
    gap = jnp.zeros((R_DEV, 256 - HALF), F32)
    wide = jnp.concatenate([embedding[:, :HALF], gap, embedding[:, HALF:], gap], axis=1)
    with_sum = jnp.concatenate(
        [embedding[:, :HALF], gap[:, 1:], adagrad[:, None], embedding[:, HALF:], gap], axis=1
    )
    vmem = pl.BlockSpec(memory_space=pltpu.VMEM)
    smem = pl.BlockSpec(memory_space=pltpu.SMEM)
    rows = (R_DEV, PART, LANES)
    panel = (NR, R_DEV, WIDE)
    half = (NX, R_DEV, WIDE)
    V = pltpu.VMEM
    result = pl.pallas_call(
        kernel,
        out_shape=jax.ShapeDtypeStruct(rows, F32),
        in_specs=[smem, smem] + [vmem] * 6 + [pl.BlockSpec(memory_space=pl.ANY)],
        out_specs=vmem,
        scratch_shapes=[
            V((NREL, D), BF16),
            V((NREL, WIDE), BF16),
            V((ROUNDS, EDGES, WIDE), BF16),
            V((EDGES, ROWS), BF16),
            V((EDGES, ROWS), BF16),
            V((ROWS, EDGES), BF16),
            V((ROWS, EDGES), BF16),
            V((EDGES, WIDE), BF16),
            V((2, EDGES, WIDE), BF16),
            V((2, EDGES, WIDE), BF16),
            V((NEG, WIDE), F32),
            V((NEG, WIDE), BF16),
            V(rows, F32),
            V(rows, BF16),
            V((4,) + rows, BF16),
            V((ROUNDS,) + rows, BF16),
            V(rows, BF16),
            V((R_DEV, WIDE), BF16),
            V((ROUNDS, R_DEV, WIDE), BF16),
            V((ROUNDS,) + panel, BF16),
            V((ROUNDS,) + panel, BF16),
            V((ROUNDS,) + panel, F32),
            V((ROUNDS,) + panel, F32),
            V((ROUNDS,) + half, F32),
            V((ROUNDS,) + half, F32),
            V((2 * ROUNDS,) + half, BF16),
            V((ROUNDS,) + half, BF16),
            V((ROUNDS,) + half, BF16),
            V((2 * ROUNDS,) + rows, BF16),
            V((ROUNDS,) + rows, BF16),
            V((ROUNDS,) + rows, BF16),
            pltpu.SemaphoreType.DMA((1,)),
            pltpu.SemaphoreType.DMA((9,)),
            pltpu.SemaphoreType.DMA((9,)),
            pltpu.SemaphoreType.DMA((4, 8)),
            pltpu.SemaphoreType.DMA((4, 8)),
            pltpu.SemaphoreType.DMA((4, 4)),
            pltpu.SemaphoreType.DMA((4, 4)),
        ],
        compiler_params=pltpu.CompilerParams(
            collective_id=0, has_side_effects=True, vmem_limit_bytes=60 * 1024 * 1024
        ),
        name="train",
    )(
        offsets,
        counts,
        with_sum.reshape(rows),
        wide.astype(BF16),
        lhs_index,
        rhs_index,
        rel_ids,
        neg_index.reshape(ROUNDS, NEG),
        relation,
    ).reshape(R_DEV, WIDE)
    embedding_out = jnp.concatenate([result[:, :HALF], result[:, 256 : 256 + HALF]], axis=1)
    return (embedding_out, result[:, 255])


def solution(mesh):
    return jax.shard_map(
        body,
        mesh=mesh,
        in_specs=(
            P(("dom", "row"), None),
            P(("dom", "row")),
            P(),
            P(),
            P(None, ("dom", "row")),
            P(None, ("dom", "row")),
            P(None, ("dom", "row")),
            P(None, ("dom", "row")),
            P(None, "dom", None),
        ),
        out_specs=(P(("dom", "row"), None), P(("dom", "row"))),
        check_vma=False,
    )
```

```python
import jax
import jax.numpy as jnp
from jax import lax
from jax.experimental import pallas as pl
from jax.experimental.pallas import tpu as pltpu
from jax.sharding import PartitionSpec as P

ROUNDS = 2
D = 400
HALF = 200
WIDE = 512
PART = 4
LANES = 128
SUM_PIECE, SUM_LANE = 1, 127
ND, NR, NX, NY, NZ = 64, 8, 4, 4, 16
R_DEV = 64
ROWS = 512
EDGES = 2048
NREL = 4096
NEG = 128
BLOCK = 256
BLOCKS = EDGES // BLOCK
STEP = 2048
STEPS = EDGES // STEP
LEARN = 0.1
MESH = pl.DeviceIdType.MESH
F32, BF16 = jnp.float32, jnp.bfloat16
NT = (((1,), (1,)), ((), ()))
TN = (((0,), (0,)), ((), ()))


def dot(a, b):
    return jnp.dot(a, b, preferred_element_type=F32)


def remote(src, dst, send, recv, device):
    return pltpu.make_async_remote_copy(
        src_ref=src, dst_ref=dst, send_sem=send, recv_sem=recv, device_id=device, device_id_type=MESH
    )


def panel_order(ids):
    owner = ids // R_DEV
    return (owner % 2) * (ROWS // 2) + (owner // 2) * R_DEV + ids % R_DEV


def as_column(row):
    return jnp.transpose(jnp.broadcast_to(row, (LANES, row.shape[1])))


def one_hot_rows(row, count):
    column = as_column(row)
    lane = lax.broadcasted_iota(jnp.int32, column.shape, 1)
    pieces = [(column == lane + first).astype(F32).astype(BF16) for first in range(0, count, LANES)]
    return jnp.concatenate(pieces, axis=1)


def one_hot_columns(row, count):
    place = lax.broadcasted_iota(jnp.int32, (count, row.shape[1]), 0)
    return (row == place).astype(F32).astype(BF16)


def split(value):
    high = value.astype(BF16)
    return high, (value - high.astype(F32)).astype(BF16)


def kernel(
    offsets, counts, embedding, adagrad, lhs, rhs, rel, neg, relation,
    out,
    raw, work0, state0, head0, home, home_t, rel_rows, hot_h, hot_t, hot_ht, hot_tt, query, tail_rows, pos_weights, neg_weights, grad_h, grad_t, neg_sum, neg_rows,
    state, work, stage, tail_in, head_in, shard_h, shard_t, panel_h, panel_t,
    acc_h, acc_t, near_h, near_t, far_send, far_h, far_t, row_send, got_h, got_t,
    raw_sem, a2a_send, a2a_recv, ag_send, ag_recv, rs_send, rs_recv,
):
    me, row = lax.axis_index("dom"), lax.axis_index("row")
    x, core = row // 2, lax.rem(row, 2)
    y, z = me // NZ, lax.rem(me, NZ)
    sibling = x * 2 + 1 - core
    slot = core * NX + x

    barrier = pltpu.get_barrier_semaphore()

    def greet(j, c):
        pl.semaphore_signal(barrier, inc=1, device_id=(lax.rem(me + j, ND), row), device_id_type=MESH)
        return c

    lax.fori_loop(1, ND, greet, 0)
    for j in range(1, NR):
        pl.semaphore_signal(barrier, inc=1, device_id=(me, lax.rem(row + j, NR)), device_id_type=MESH)

    gap = jnp.zeros((R_DEV, 256 - HALF), F32)
    wide = jnp.concatenate([embedding[:, :HALF], gap, embedding[:, HALF:], gap], axis=1)
    column = lax.broadcasted_iota(jnp.int32, (R_DEV, WIDE), 1)
    sums = as_column(jnp.concatenate([adagrad[...], adagrad[...]], axis=1))[:R_DEV, :1]
    state0[...] = jnp.where(column == SUM_PIECE * LANES + SUM_LANE, sums, wide).reshape(state0.shape)
    head0[...] = wide.astype(BF16)
    work0[...] = wide.reshape(work0.shape).astype(BF16)

    def relation_block(k, b):
        at = pl.ds(pl.multiple_of(b * BLOCK, BLOCK), BLOCK)
        found = dot(raw[...], one_hot_columns(rel[pl.ds(k, 1), at], NREL))
        hole = jnp.zeros((256 - HALF, BLOCK), F32)
        spaced = jnp.concatenate([found[:HALF], hole, found[HALF:], hole], axis=0)
        rel_rows[k, at, :] = jnp.transpose(spaced).astype(BF16)

    def relation_blocks(k, first, last):
        def step(b, c):
            relation_block(k, b)
            return c

        lax.fori_loop(first, last, step, 0)

    def selectors(k):
        def step(b, c):
            at = pl.ds(pl.multiple_of(b * BLOCK, BLOCK), BLOCK)
            head_ids = panel_order(lhs[pl.ds(k, 1), at])
            tail_ids = panel_order(rhs[pl.ds(k, 1), at])
            hot_h[at, :] = one_hot_rows(head_ids, ROWS)
            hot_t[at, :] = one_hot_rows(tail_ids, ROWS)
            hot_ht[:, at] = one_hot_columns(head_ids, ROWS)
            hot_tt[:, at] = one_hot_columns(tail_ids, ROWS)
            return c

        lax.fori_loop(0, BLOCKS, step, 0)

    def queries(k):
        panel = panel_h[k].reshape(ROWS, WIDE)

        def step(b, c):
            at = pl.ds(pl.multiple_of(b * STEP, STEP), STEP)
            heads = dot(hot_h[at, :], panel)
            rels = rel_rows[k, at, :].astype(F32)
            h_re, h_im = heads[:, :256], heads[:, 256:]
            c_re, c_im = rels[:, :256], rels[:, 256:]
            query[at, :256] = (h_re * c_re - h_im * c_im).astype(BF16)
            query[at, 256:] = (h_re * c_im + h_im * c_re).astype(BF16)
            return c

        lax.fori_loop(0, STEPS, step, 0)

    def tail_grads(k):
        panel = panel_t[k].reshape(ROWS, WIDE)
        neg_ids = panel_order(neg[pl.ds(k, 1), :])
        negatives = dot(one_hot_rows(neg_ids, ROWS), panel)
        neg_rows[...] = negatives.astype(BF16)
        neg_turned = jnp.transpose(negatives).astype(BF16)
        neg_sum[...] = jnp.zeros_like(neg_sum)
        count = counts[k]

        def step(b, c):
            at = pl.ds(pl.multiple_of(b * STEP, STEP), STEP)
            tails = dot(hot_t[at, :], panel)
            tail_rows[at, :] = tails.astype(BF16)
            q = query[at, :]
            q_f = q.astype(F32)
            positive = jnp.sum(q_f * tails, axis=1, keepdims=True)
            negative = dot(q, neg_turned)
            live = b * STEP + lax.broadcasted_iota(jnp.int32, (STEP, 1), 0) < count
            pos_weight = jnp.where(live, -1.0 / (1.0 + jnp.exp(positive)), 0.0)
            neg_weight = jnp.where(live, (1.0 / NEG) / (1.0 + jnp.exp(-negative)), 0.0).astype(BF16)
            pos_weights[at, :] = pos_weight
            neg_weights[at, :] = neg_weight
            high, low = split(pos_weight * q_f)
            grad_t[0, at, :] = high
            grad_t[1, at, :] = low
            neg_sum[...] += lax.dot_general(neg_weight, q, TN, preferred_element_type=F32)
            return c

        lax.fori_loop(0, STEPS, step, 0)

    def head_grads(k):
        def step(b, c):
            at = pl.ds(pl.multiple_of(b * STEP, STEP), STEP)
            g = pos_weights[at, :] * tail_rows[at, :].astype(F32) + dot(neg_weights[at, :], neg_rows[...])
            rels = rel_rows[k, at, :].astype(F32)
            g_re, g_im = g[:, :256], g[:, 256:]
            c_re, c_im = rels[:, :256], rels[:, 256:]
            high, low = split(g_re * c_re + g_im * c_im)
            grad_h[0, at, :256] = high
            grad_h[1, at, :256] = low
            high, low = split(g_im * c_re - g_re * c_im)
            grad_h[0, at, 256:] = high
            grad_h[1, at, 256:] = low
            return c

        lax.fori_loop(0, STEPS, step, 0)

    def tail_sums(k, half):
        rows = pl.ds(half * (ROWS // 2), ROWS // 2)
        hot_n = one_hot_columns(panel_order(neg[pl.ds(k, 1), :]) - half * (ROWS // 2), ROWS // 2)
        high, low = split(neg_sum[...])
        total = dot(hot_tt[rows, :], grad_t[0]) + dot(hot_tt[rows, :], grad_t[1]) + dot(hot_n, high) + dot(hot_n, low)
        acc_t[k, pl.ds(half * NX, NX)] = total.reshape(NX, R_DEV, WIDE)

    def head_sums(k, half):
        rows = pl.ds(half * (ROWS // 2), ROWS // 2)
        total = dot(hot_ht[rows, :], grad_h[0]) + dot(hot_ht[rows, :], grad_h[1])
        acc_h[k, pl.ds(half * NX, NX)] = total.reshape(NX, R_DEV, WIDE)

    def spread(number, src, dst):
        def send(dy, dz):
            t = lax.rem(y + dy, NY) * NZ + lax.rem(z + dz, NZ)
            remote(src.at[t], dst.at[me], a2a_send.at[number], a2a_recv.at[number], (t, row)).start()

        def step(i, c):
            dz = NZ // 2 + (i + 1) // 2 * (1 - 2 * (i % 2))
            for dy in (2, 1, 3, 0):
                send(dy, dz)
            return c

        lax.fori_loop(0, NZ - 1, step, 0)
        for dy in (2, 1, 3):
            send(dy, 0)
        dst[me] = src[me]

    def spread_wait(number, src, dst):
        most = pl.ds(0, ND - 1)
        remote(src.at[most], dst.at[most], a2a_send.at[number], a2a_recv.at[number], (lax.rem(me + 1, ND), row)).wait()

    def rotated(k, src, dst, forward):
        by = offsets[k]
        shift = by if forward else ND - by

        def step(j, c):
            dst[j] = src[lax.rem(j + shift, ND)]
            return c

        lax.fori_loop(0, ND, step, 0)

    def gather_far(number, src, panel):
        copies = []
        for j in (2, 1, 3):
            t = lax.rem(x + j, NX) * 2 + core
            copies.append(remote(src, panel.at[slot], ag_send.at[number, j], ag_recv.at[number, j], (me, t)))
        return copies

    def gather_near(number, src, panel):
        return remote(src, panel.at[slot], ag_send.at[number, 0], ag_recv.at[number, 0], (me, sibling))

    def gather_start(number, src, panel):
        for copy in gather_far(number, src, panel):
            copy.start()
        gather_near(number, src, panel).start()
        panel[slot] = src[...]

    def gather_passed(number, panel):
        copies = []
        for j in (1, 3, 2):
            place = core * NX + lax.rem(x + NX - j, NX)
            copies.append(
                remote(
                    panel.at[place], panel.at[place], ag_send.at[number, NX + j], ag_recv.at[number, NX + j], (me, sibling)
                )
            )
        return copies

    def gather_pass(number, src, panel):
        opposite, right, left = gather_far(number, src, panel)
        for came, onward in zip((right, left, opposite), gather_passed(number, panel)):
            came.wait_recv()
            onward.start()

    def gather_end(number, src, panel):
        for copy in gather_far(number, src, panel):
            copy.wait_send()
        gather_near(number, src, panel).wait()
        for copy in gather_passed(number, panel):
            copy.wait()

    def near_copy(number, acc, near):
        other = pl.ds((1 - core) * NX, NX)
        return remote(acc.at[other], near, rs_send.at[number, 0], rs_recv.at[number, 0], (me, sibling))

    def far_copies(number, far):
        copies = []
        for j in (2, 1, 3):
            t = lax.rem(x + j, NX)
            copies.append(
                remote(
                    far_send.at[number, t], far.at[j], rs_send.at[number, j], rs_recv.at[number, j], (me, t * 2 + core)
                )
            )
        return copies

    def sum_near(number, acc, near, far):
        near_copy(number, acc, near).wait()
        near[...] = near[...] + acc[pl.ds(core * NX, NX)]
        far_send[number] = near[...].astype(BF16)
        for copy in far_copies(number, far):
            copy.start()

    def sum_far(number, near, far):
        for copy in far_copies(number, far):
            copy.wait()
        return near[x] + (far[1].astype(F32) + far[2].astype(F32) + far[3].astype(F32))

    def is_sum():
        piece = lax.broadcasted_iota(jnp.int32, state.shape, 1)
        lane = lax.broadcasted_iota(jnp.int32, state.shape, 2)
        return (piece == SUM_PIECE) & (lane == SUM_LANE)

    def update(k):
        rotated(k, got_t.at[k], stage.at[2 + k], False)
        gradient = got_h[...].astype(F32) + stage[2 + k].astype(F32)
        at_sum = is_sum()
        now = state[...]
        squares = jnp.sum(jnp.where(at_sum, now, 0.0), axis=(1, 2), keepdims=True)
        squares = squares + jnp.sum(gradient * gradient, axis=(1, 2), keepdims=True) / D
        state[...] = jnp.where(at_sum, squares, now - LEARN * gradient / jnp.sqrt(squares))

    def finish(head_sum):
        gradient = head_sum + home_t[...].astype(F32).reshape(R_DEV, WIDE)
        now = home[...].reshape(R_DEV, WIDE)
        place = SUM_PIECE * LANES + SUM_LANE
        squares = now[:, place : place + 1] + jnp.sum(gradient * gradient, axis=1, keepdims=True) / D
        now = now - LEARN * gradient / jnp.sqrt(squares)
        column = lax.broadcasted_iota(jnp.int32, now.shape, 1)
        out[...] = jnp.where(column == place, squares, now)

    def to_rows(value):
        return value.reshape(R_DEV, PART, LANES).astype(BF16)

    def to_shard(value):
        return value.astype(F32).reshape(R_DEV, WIDE).astype(BF16)

    fetch = pltpu.make_async_copy(relation, raw, raw_sem.at[0])
    fetch.start()
    selectors(0)
    fetch.wait()
    relation_blocks(0, 0, 2)

    pl.semaphore_wait(barrier, ND - 1 + NR - 1)
    spread(0, work0, work)
    gather_start(0, head0, panel_h.at[0])
    relation_blocks(0, 2, 5)
    gather_pass(0, head0, panel_h.at[0])
    relation_blocks(0, 5, 7)
    spread_wait(0, work0, work)
    rotated(0, work, stage.at[0], True)
    spread(1, stage.at[0], tail_in.at[0])
    relation_blocks(0, 7, 8)
    gather_end(0, head0, panel_h.at[0])
    queries(0)
    spread_wait(1, stage.at[0], tail_in.at[0])
    shard_t[0] = to_shard(tail_in[0])
    gather_start(1, shard_t.at[0], panel_t.at[0])
    spread(9, state0, state)
    relation_blocks(1, 0, 2)
    gather_pass(1, shard_t.at[0], panel_t.at[0])
    relation_blocks(1, 2, 3)
    gather_end(1, shard_t.at[0], panel_t.at[0])

    for k in range(ROUNDS):
        last = k == ROUNDS - 1
        if k > 0:
            spread_wait(4, work, head_in)
            shard_h[...] = to_shard(head_in[...])
            gather_start(2, shard_h, panel_h.at[1])
            spread_wait(5, stage.at[1], tail_in.at[1])
            shard_t[1] = to_shard(tail_in[1])
            gather_start(3, shard_t.at[1], panel_t.at[1])
            gather_pass(2, shard_h, panel_h.at[1])
            gather_end(2, shard_h, panel_h.at[1])
            gather_pass(3, shard_t.at[1], panel_t.at[1])
            queries(1)
            gather_end(3, shard_t.at[1], panel_t.at[1])
        tail_grads(k)
        tail_sums(k, 1 - core)
        near_copy(2 * k, acc_t.at[k], near_t.at[k]).start()
        tail_sums(k, core)
        head_grads(k)
        sum_near(2 * k, acc_t.at[k], near_t.at[k], far_t.at[k])
        head_sums(k, 1 - core)
        near_copy(2 * k + 1, acc_h.at[k], near_h.at[k]).start()
        head_sums(k, core)
        if not last:
            relation_blocks(1, 3, 4)
        sum_near(2 * k + 1, acc_h.at[k], near_h.at[k], far_h.at[k])
        row_send[2 * k] = to_rows(sum_far(2 * k, near_t.at[k], far_t.at[k]))
        spread(2 + 4 * k, row_send.at[2 * k], got_t.at[k])
        if not last:
            relation_blocks(1, 4, 6)
            row_send[1] = to_rows(sum_far(1, near_h.at[0], far_h.at[0]))
            spread(3, row_send.at[1], got_h)
            relation_blocks(1, 6, 8)
            selectors(1)
            spread_wait(9, state0, state)
            spread_wait(2, row_send.at[0], got_t.at[0])
            spread_wait(3, row_send.at[1], got_h)
            update(0)
            work[...] = jnp.where(is_sum(), 0.0, state[...]).astype(BF16)
            spread(4, work, head_in)
            rotated(1, work, stage.at[1], True)
            spread(5, stage.at[1], tail_in.at[1])
            spread(7, state, home)
        else:
            head_sum = sum_far(2 * k + 1, near_h.at[k], far_h.at[k])
            spread_wait(7, state, home)
            spread_wait(6, row_send.at[2], got_t.at[1])
            rotated(1, got_t.at[1], stage.at[3], False)
            spread(8, stage.at[3], home_t)
            spread_wait(8, stage.at[3], home_t)
            finish(head_sum)


def narrow(state, embedding_out, adagrad_out):
    now = state[...]
    embedding_out[...] = jnp.concatenate([now[:, :HALF], now[:, 256 : 256 + HALF]], axis=1)
    place = SUM_PIECE * LANES + SUM_LANE
    squares = jnp.broadcast_to(now[:, place : place + 1], (R_DEV, LANES))
    adagrad_out[...] = jnp.transpose(jnp.concatenate([squares, squares], axis=0))[:1, :R_DEV]


def body(embedding, adagrad, relation, offsets, counts, lhs_index, rhs_index, rel_ids, neg_index):
    vmem = pl.BlockSpec(memory_space=pltpu.VMEM)
    smem = pl.BlockSpec(memory_space=pltpu.SMEM)
    rows = (R_DEV, PART, LANES)
    panel = (NR, R_DEV, WIDE)
    half = (NX, R_DEV, WIDE)
    V = pltpu.VMEM
    state = pl.pallas_call(
        kernel,
        out_shape=jax.ShapeDtypeStruct((R_DEV, WIDE), F32),
        in_specs=[smem, smem] + [vmem] * 6 + [pl.BlockSpec(memory_space=pl.ANY)],
        out_specs=vmem,
        scratch_shapes=[
            V((D, NREL), BF16),
            V(rows, BF16),
            V(rows, F32),
            V((R_DEV, WIDE), BF16),
            V(rows, F32),
            V(rows, BF16),
            V((ROUNDS, EDGES, WIDE), BF16),
            V((EDGES, ROWS), BF16),
            V((EDGES, ROWS), BF16),
            V((ROWS, EDGES), BF16),
            V((ROWS, EDGES), BF16),
            V((EDGES, WIDE), BF16),
            V((EDGES, WIDE), BF16),
            V((EDGES, 1), F32),
            V((EDGES, NEG), BF16),
            V((2, EDGES, WIDE), BF16),
            V((2, EDGES, WIDE), BF16),
            V((NEG, WIDE), F32),
            V((NEG, WIDE), BF16),
            V(rows, F32),
            V(rows, BF16),
            V((4,) + rows, BF16),
            V((ROUNDS,) + rows, BF16),
            V(rows, BF16),
            V((R_DEV, WIDE), BF16),
            V((ROUNDS, R_DEV, WIDE), BF16),
            V((ROUNDS,) + panel, BF16),
            V((ROUNDS,) + panel, BF16),
            V((ROUNDS,) + panel, F32),
            V((ROUNDS,) + panel, F32),
            V((ROUNDS,) + half, F32),
            V((ROUNDS,) + half, F32),
            V((2 * ROUNDS,) + half, BF16),
            V((ROUNDS,) + half, BF16),
            V((ROUNDS,) + half, BF16),
            V((3,) + rows, BF16),
            V(rows, BF16),
            V((ROUNDS,) + rows, BF16),
            pltpu.SemaphoreType.DMA((1,)),
            pltpu.SemaphoreType.DMA((10,)),
            pltpu.SemaphoreType.DMA((10,)),
            pltpu.SemaphoreType.DMA((4, 8)),
            pltpu.SemaphoreType.DMA((4, 8)),
            pltpu.SemaphoreType.DMA((4, 4)),
            pltpu.SemaphoreType.DMA((4, 4)),
        ],
        compiler_params=pltpu.CompilerParams(
            collective_id=0, has_side_effects=True, vmem_limit_bytes=60 * 1024 * 1024
        ),
        name="train",
    )(
        offsets,
        counts.reshape(ROUNDS),
        embedding,
        adagrad.reshape(1, R_DEV),
        lhs_index,
        rhs_index,
        rel_ids,
        neg_index.reshape(ROUNDS, NEG),
        relation.T,
    )
    embedding_out, adagrad_out = pl.pallas_call(
        narrow,
        out_shape=[jax.ShapeDtypeStruct((R_DEV, D), F32), jax.ShapeDtypeStruct((1, R_DEV), F32)],
        in_specs=[vmem],
        out_specs=[vmem, vmem],
        name="narrow",
    )(state)
    return (embedding_out, adagrad_out.reshape(R_DEV))


def solution(mesh):
    return jax.shard_map(
        body,
        mesh=mesh,
        in_specs=(
            P(("dom", "row"), None),
            P(("dom", "row")),
            P(),
            P(),
            P(None, ("dom", "row")),
            P(None, ("dom", "row")),
            P(None, ("dom", "row")),
            P(None, ("dom", "row")),
            P(None, "dom", None),
        ),
        out_specs=(P(("dom", "row"), None), P(("dom", "row"))),
        check_vma=False,
    )
```

```python
import jax
import jax.numpy as jnp
from jax import lax
from jax.experimental import pallas as pl
from jax.experimental.pallas import tpu as pltpu
from jax.sharding import PartitionSpec as P

ROUNDS = 2
D = 400
HALF = 200
WIDE = 512
PART = 4
LANES = 128
SUM_PIECE, SUM_LANE = 1, 127
ND, NR, NX, NY, NZ = 64, 8, 4, 4, 16
R_DEV = 64
ROWS = 512
EDGES = 2048
NREL = 4096
NEG = 128
BLOCK = 256
BLOCKS = EDGES // BLOCK
STEP = 2048
STEPS = EDGES // STEP
LEARN = 0.1
MESH = pl.DeviceIdType.MESH
F32, BF16 = jnp.float32, jnp.bfloat16
NT = (((1,), (1,)), ((), ()))
TN = (((0,), (0,)), ((), ()))


def dot(a, b):
    return jnp.dot(a, b, preferred_element_type=F32)


def remote(src, dst, send, recv, device):
    return pltpu.make_async_remote_copy(
        src_ref=src, dst_ref=dst, send_sem=send, recv_sem=recv, device_id=device, device_id_type=MESH
    )


def panel_order(ids):
    owner = ids // R_DEV
    return (owner % 2) * (ROWS // 2) + (owner // 2) * R_DEV + ids % R_DEV


def as_column(row):
    return jnp.transpose(jnp.broadcast_to(row, (LANES, row.shape[1])))


def one_hot_rows(row, count):
    column = as_column(row)
    lane = lax.broadcasted_iota(jnp.int32, column.shape, 1)
    pieces = [(column == lane + first).astype(F32).astype(BF16) for first in range(0, count, LANES)]
    return jnp.concatenate(pieces, axis=1)


def one_hot_columns(row, count):
    place = lax.broadcasted_iota(jnp.int32, (count, row.shape[1]), 0)
    return (row == place).astype(F32).astype(BF16)


def split(value):
    high = value.astype(BF16)
    return high, (value - high.astype(F32)).astype(BF16)


def kernel(
    offsets, counts, embedding_in, adagrad_in, lhs_in, rhs_in, rel_in, neg_in, relation,
    out,
    embedding, adagrad, lhs, rhs, rel, neg, raw, work0, state0, head0, home, home_t, rel_rows, hot_h, hot_t, hot_ht, hot_tt, query, tail_rows, pos_weights, neg_weights, grad_h, grad_t, neg_sum, neg_rows,
    state, work, stage, tail_in, head_in, shard_h, shard_t, panel_h, panel_t,
    acc_h, acc_t, near_h, near_t, far_send, far_h, far_t, row_send, got_h, got_t,
    raw_sem, a2a_send, a2a_recv, ag_send, ag_recv, rs_send, rs_recv,
):
    me, row = lax.axis_index("dom"), lax.axis_index("row")
    x, core = row // 2, lax.rem(row, 2)
    y, z = me // NZ, lax.rem(me, NZ)
    sibling = x * 2 + 1 - core
    slot = core * NX + x

    barrier = pltpu.get_barrier_semaphore()

    def over_dom(act):
        def step(i, c):
            dz = NZ // 2 + (i + 1) // 2 * (1 - 2 * (i % 2))
            for dy in (2, 1, 3, 0):
                act(lax.rem(y + dy, NY) * NZ + lax.rem(z + dz, NZ))
            return c

        lax.fori_loop(0, NZ - 1, step, 0)
        for dy in (2, 1, 3):
            act(lax.rem(y + dy, NY) * NZ + z)

    over_dom(lambda t: pl.semaphore_signal(barrier, inc=1, device_id=(t, row), device_id_type=MESH))
    for j in range(1, NR):
        pl.semaphore_signal(barrier, inc=1, device_id=(me, lax.rem(row + j, NR)), device_id_type=MESH)

    fetches = [
        pltpu.make_async_copy(src, dst, raw_sem.at[number])
        for number, (src, dst) in enumerate(
            [
                (embedding_in, embedding),
                (adagrad_in, adagrad),
                (lhs_in, lhs),
                (rhs_in, rhs),
                (rel_in, rel),
                (neg_in, neg),
                (relation, raw),
            ]
        )
    ]
    for fetch in fetches:
        fetch.start()
    for fetch in fetches[:-1]:
        fetch.wait()

    gap = jnp.zeros((R_DEV, 256 - HALF), F32)
    wide = jnp.concatenate([embedding[:, :HALF], gap, embedding[:, HALF:], gap], axis=1)
    column = lax.broadcasted_iota(jnp.int32, (R_DEV, WIDE), 1)
    sums = as_column(jnp.concatenate([adagrad[...], adagrad[...]], axis=1))[:R_DEV, :1]
    state0[...] = jnp.where(column == SUM_PIECE * LANES + SUM_LANE, sums, wide).reshape(state0.shape)
    head0[...] = wide.astype(BF16)
    work0[...] = wide.reshape(work0.shape).astype(BF16)

    def relation_block(k, b):
        at = pl.ds(pl.multiple_of(b * BLOCK, BLOCK), BLOCK)
        found = dot(raw[...], one_hot_columns(rel[pl.ds(k, 1), at], NREL))
        hole = jnp.zeros((256 - HALF, BLOCK), F32)
        spaced = jnp.concatenate([found[:HALF], hole, found[HALF:], hole], axis=0)
        rel_rows[k, at, :] = jnp.transpose(spaced).astype(BF16)

    def relation_blocks(k, first, last):
        def step(b, c):
            relation_block(k, b)
            return c

        lax.fori_loop(first, last, step, 0)

    def selectors(k):
        def step(b, c):
            at = pl.ds(pl.multiple_of(b * BLOCK, BLOCK), BLOCK)
            head_ids = panel_order(lhs[pl.ds(k, 1), at])
            tail_ids = panel_order(rhs[pl.ds(k, 1), at])
            hot_h[at, :] = one_hot_rows(head_ids, ROWS)
            hot_t[at, :] = one_hot_rows(tail_ids, ROWS)
            hot_ht[:, at] = one_hot_columns(head_ids, ROWS)
            hot_tt[:, at] = one_hot_columns(tail_ids, ROWS)
            return c

        lax.fori_loop(0, BLOCKS, step, 0)

    def queries(k):
        panel = panel_h[k].reshape(ROWS, WIDE)

        def step(b, c):
            at = pl.ds(pl.multiple_of(b * STEP, STEP), STEP)
            heads = dot(hot_h[at, :], panel)
            rels = rel_rows[k, at, :].astype(F32)
            h_re, h_im = heads[:, :256], heads[:, 256:]
            c_re, c_im = rels[:, :256], rels[:, 256:]
            query[at, :256] = (h_re * c_re - h_im * c_im).astype(BF16)
            query[at, 256:] = (h_re * c_im + h_im * c_re).astype(BF16)
            return c

        lax.fori_loop(0, STEPS, step, 0)

    def tail_grads(k):
        panel = panel_t[k].reshape(ROWS, WIDE)
        neg_ids = panel_order(neg[pl.ds(k, 1), :])
        negatives = dot(one_hot_rows(neg_ids, ROWS), panel)
        neg_rows[...] = negatives.astype(BF16)
        neg_turned = jnp.transpose(negatives).astype(BF16)
        neg_sum[...] = jnp.zeros_like(neg_sum)
        count = counts[k]

        def step(b, c):
            at = pl.ds(pl.multiple_of(b * STEP, STEP), STEP)
            tails = dot(hot_t[at, :], panel)
            tail_rows[at, :] = tails.astype(BF16)
            q = query[at, :]
            q_f = q.astype(F32)
            positive = jnp.sum(q_f * tails, axis=1, keepdims=True)
            negative = dot(q, neg_turned)
            live = b * STEP + lax.broadcasted_iota(jnp.int32, (STEP, 1), 0) < count
            pos_weight = jnp.where(live, -1.0 / (1.0 + jnp.exp(positive)), 0.0)
            neg_weight = jnp.where(live, (1.0 / NEG) / (1.0 + jnp.exp(-negative)), 0.0).astype(BF16)
            pos_weights[at, :] = pos_weight
            neg_weights[at, :] = neg_weight
            high, low = split(pos_weight * q_f)
            grad_t[0, at, :] = high
            grad_t[1, at, :] = low
            neg_sum[...] += lax.dot_general(neg_weight, q, TN, preferred_element_type=F32)
            return c

        lax.fori_loop(0, STEPS, step, 0)

    def head_grads(k):
        def step(b, c):
            at = pl.ds(pl.multiple_of(b * STEP, STEP), STEP)
            g = pos_weights[at, :] * tail_rows[at, :].astype(F32) + dot(neg_weights[at, :], neg_rows[...])
            rels = rel_rows[k, at, :].astype(F32)
            g_re, g_im = g[:, :256], g[:, 256:]
            c_re, c_im = rels[:, :256], rels[:, 256:]
            high, low = split(g_re * c_re + g_im * c_im)
            grad_h[0, at, :256] = high
            grad_h[1, at, :256] = low
            high, low = split(g_im * c_re - g_re * c_im)
            grad_h[0, at, 256:] = high
            grad_h[1, at, 256:] = low
            return c

        lax.fori_loop(0, STEPS, step, 0)

    def tail_sums(k, half):
        rows = pl.ds(half * (ROWS // 2), ROWS // 2)
        hot_n = one_hot_columns(panel_order(neg[pl.ds(k, 1), :]) - half * (ROWS // 2), ROWS // 2)
        high, low = split(neg_sum[...])
        total = dot(hot_tt[rows, :], grad_t[0]) + dot(hot_tt[rows, :], grad_t[1]) + dot(hot_n, high) + dot(hot_n, low)
        acc_t[k, pl.ds(half * NX, NX)] = total.reshape(NX, R_DEV, WIDE)

    def head_sums(k, half):
        rows = pl.ds(half * (ROWS // 2), ROWS // 2)
        total = dot(hot_ht[rows, :], grad_h[0]) + dot(hot_ht[rows, :], grad_h[1])
        acc_h[k, pl.ds(half * NX, NX)] = total.reshape(NX, R_DEV, WIDE)

    def spread(number, src, dst):
        def send(t):
            remote(src.at[t], dst.at[me], a2a_send.at[number], a2a_recv.at[number], (t, row)).start()

        over_dom(send)
        dst[me] = src[me]

    def spread_wait(number, src, dst):
        most = pl.ds(0, ND - 1)
        remote(src.at[most], dst.at[most], a2a_send.at[number], a2a_recv.at[number], (lax.rem(me + 1, ND), row)).wait()

    def rotated(k, src, dst, forward):
        by = offsets[k]
        shift = by if forward else ND - by

        def step(j, c):
            dst[j] = src[lax.rem(j + shift, ND)]
            return c

        lax.fori_loop(0, ND, step, 0, unroll=8)

    def gather_far(number, src, panel):
        copies = []
        for j in (2, 1, 3):
            t = lax.rem(x + j, NX) * 2 + core
            copies.append(remote(src, panel.at[slot], ag_send.at[number, j], ag_recv.at[number, j], (me, t)))
        return copies

    def gather_near(number, src, panel):
        return remote(src, panel.at[slot], ag_send.at[number, 0], ag_recv.at[number, 0], (me, sibling))

    def gather_start(number, src, panel):
        for copy in gather_far(number, src, panel):
            copy.start()
        gather_near(number, src, panel).start()
        panel[slot] = src[...]

    def gather_passed(number, panel):
        copies = []
        for j in (1, 3, 2):
            place = core * NX + lax.rem(x + NX - j, NX)
            copies.append(
                remote(
                    panel.at[place], panel.at[place], ag_send.at[number, NX + j], ag_recv.at[number, NX + j], (me, sibling)
                )
            )
        return copies

    def gather_pass(number, src, panel):
        opposite, right, left = gather_far(number, src, panel)
        for came, onward in zip((right, left, opposite), gather_passed(number, panel)):
            came.wait_recv()
            onward.start()

    def gather_end(number, src, panel):
        for copy in gather_far(number, src, panel):
            copy.wait_send()
        gather_near(number, src, panel).wait()
        for copy in gather_passed(number, panel):
            copy.wait()

    def near_copy(number, acc, near):
        other = pl.ds((1 - core) * NX, NX)
        return remote(acc.at[other], near, rs_send.at[number, 0], rs_recv.at[number, 0], (me, sibling))

    def far_copies(number, far):
        copies = []
        for j in (2, 1, 3):
            t = lax.rem(x + j, NX)
            copies.append(
                remote(
                    far_send.at[number, t], far.at[j], rs_send.at[number, j], rs_recv.at[number, j], (me, t * 2 + core)
                )
            )
        return copies

    def sum_near(copy, number, acc, near, far):
        copy.wait()
        near[...] = near[...] + acc[pl.ds(core * NX, NX)]
        far_send[number] = near[...].astype(BF16)
        for copy in far_copies(number, far):
            copy.start()

    def sum_far(number, near, far):
        for copy in far_copies(number, far):
            copy.wait()
        return near[x] + (far[1].astype(F32) + far[2].astype(F32) + far[3].astype(F32))

    def is_sum():
        piece = lax.broadcasted_iota(jnp.int32, state.shape, 1)
        lane = lax.broadcasted_iota(jnp.int32, state.shape, 2)
        return (piece == SUM_PIECE) & (lane == SUM_LANE)

    def update(k):
        rotated(k, got_t.at[k], stage.at[2 + k], False)
        gradient = got_h[...].astype(F32) + stage[2 + k].astype(F32)
        at_sum = is_sum()
        now = state[...]
        squares = jnp.sum(jnp.where(at_sum, now, 0.0), axis=(1, 2), keepdims=True)
        squares = squares + jnp.sum(gradient * gradient, axis=(1, 2), keepdims=True) / D
        state[...] = jnp.where(at_sum, squares, now - LEARN * gradient / jnp.sqrt(squares))

    def finish(head_sum):
        gradient = head_sum + home_t[...].astype(F32).reshape(R_DEV, WIDE)
        now = home[...].reshape(R_DEV, WIDE)
        place = SUM_PIECE * LANES + SUM_LANE
        squares = now[:, place : place + 1] + jnp.sum(gradient * gradient, axis=1, keepdims=True) / D
        now = now - LEARN * gradient / jnp.sqrt(squares)
        column = lax.broadcasted_iota(jnp.int32, now.shape, 1)
        out[...] = jnp.where(column == place, squares, now)

    def to_rows(value):
        return value.reshape(R_DEV, PART, LANES).astype(BF16)

    def to_shard(value):
        return value.astype(F32).reshape(R_DEV, WIDE).astype(BF16)

    selectors(0)
    fetches[-1].wait()
    relation_blocks(0, 0, 2)

    pl.semaphore_wait(barrier, ND - 1 + NR - 1)
    spread(0, work0, work)
    gather_start(0, head0, panel_h.at[0])
    relation_blocks(0, 2, 5)
    gather_pass(0, head0, panel_h.at[0])
    relation_blocks(0, 5, 7)
    spread_wait(0, work0, work)
    rotated(0, work, stage.at[0], True)
    spread(1, stage.at[0], tail_in.at[0])
    relation_blocks(0, 7, 8)
    gather_end(0, head0, panel_h.at[0])
    queries(0)
    spread_wait(1, stage.at[0], tail_in.at[0])
    shard_t[0] = to_shard(tail_in[0])
    gather_start(1, shard_t.at[0], panel_t.at[0])
    spread(9, state0, state)
    relation_blocks(1, 0, 2)
    gather_pass(1, shard_t.at[0], panel_t.at[0])
    relation_blocks(1, 2, 3)
    gather_end(1, shard_t.at[0], panel_t.at[0])

    for k in range(ROUNDS):
        last = k == ROUNDS - 1
        if k > 0:
            spread_wait(4, work, head_in)
            shard_h[...] = to_shard(head_in[...])
            gather_start(2, shard_h, panel_h.at[1])
            spread_wait(5, stage.at[1], tail_in.at[1])
            shard_t[1] = to_shard(tail_in[1])
            gather_start(3, shard_t.at[1], panel_t.at[1])
            spread(7, state, home)
            gather_pass(2, shard_h, panel_h.at[1])
            gather_pass(3, shard_t.at[1], panel_t.at[1])
            gather_end(2, shard_h, panel_h.at[1])
            queries(1)
            gather_end(3, shard_t.at[1], panel_t.at[1])
        near_tail, near_head = (near_copy(2 * k, acc_t.at[k], near_t.at[k]), near_copy(2 * k + 1, acc_h.at[k], near_h.at[k]))
        tail_grads(k)
        if not last:
            head_grads(k)
            tail_sums(k, 1 - core)
            near_tail.start()
            head_sums(k, 1 - core)
            near_head.start()
            tail_sums(k, core)
            sum_near(near_tail, 2 * k, acc_t.at[k], near_t.at[k], far_t.at[k])
            head_sums(k, core)
            sum_near(near_head, 2 * k + 1, acc_h.at[k], near_h.at[k], far_h.at[k])
            relation_blocks(1, 3, 5)
            row_send[0] = to_rows(sum_far(0, near_t.at[0], far_t.at[0]))
            spread(2, row_send.at[0], got_t.at[0])
            row_send[1] = to_rows(sum_far(1, near_h.at[0], far_h.at[0]))
            spread(3, row_send.at[1], got_h)
            relation_blocks(1, 5, 8)
            selectors(1)
            spread_wait(9, state0, state)
            spread_wait(2, row_send.at[0], got_t.at[0])
            spread_wait(3, row_send.at[1], got_h)
            update(0)
            work[...] = jnp.where(is_sum(), 0.0, state[...]).astype(BF16)
            spread(4, work, head_in)
            rotated(1, work, stage.at[1], True)
            spread(5, stage.at[1], tail_in.at[1])
        else:
            tail_sums(k, 1 - core)
            near_tail.start()
            tail_sums(k, core)
            sum_near(near_tail, 2 * k, acc_t.at[k], near_t.at[k], far_t.at[k])
            head_grads(k)
            head_sums(k, 1 - core)
            head_sums(k, core)
            row_send[2] = to_rows(sum_far(2, near_t.at[1], far_t.at[1]))
            spread(6, row_send.at[2], got_t.at[1])
            near_head.start()
            sum_near(near_head, 2 * k + 1, acc_h.at[k], near_h.at[k], far_h.at[k])
            head_sum = sum_far(2 * k + 1, near_h.at[k], far_h.at[k])
            spread_wait(7, state, home)
            spread_wait(6, row_send.at[2], got_t.at[1])
            rotated(1, got_t.at[1], stage.at[3], False)
            spread(8, stage.at[3], home_t)
            spread_wait(8, stage.at[3], home_t)
            finish(head_sum)


def narrow(state, embedding_out, adagrad_out):
    now = state[...]
    embedding_out[...] = jnp.concatenate([now[:, :HALF], now[:, 256 : 256 + HALF]], axis=1)
    place = SUM_PIECE * LANES + SUM_LANE
    squares = jnp.broadcast_to(now[:, place : place + 1], (R_DEV, LANES))
    adagrad_out[...] = jnp.transpose(jnp.concatenate([squares, squares], axis=0))[:1, :R_DEV]


def body(embedding, adagrad, relation, offsets, counts, lhs_index, rhs_index, rel_ids, neg_index):
    vmem = pl.BlockSpec(memory_space=pltpu.VMEM)
    smem = pl.BlockSpec(memory_space=pltpu.SMEM)
    rows = (R_DEV, PART, LANES)
    panel = (NR, R_DEV, WIDE)
    half = (NX, R_DEV, WIDE)
    V = pltpu.VMEM
    state = pl.pallas_call(
        kernel,
        out_shape=jax.ShapeDtypeStruct((R_DEV, WIDE), F32),
        in_specs=[smem, smem] + [pl.BlockSpec(memory_space=pl.ANY)] * 7,
        out_specs=vmem,
        scratch_shapes=[
            V((R_DEV, D), F32),
            V((1, R_DEV), F32),
            V((ROUNDS, EDGES), jnp.int32),
            V((ROUNDS, EDGES), jnp.int32),
            V((ROUNDS, EDGES), jnp.int32),
            V((ROUNDS, NEG), jnp.int32),
            V((D, NREL), BF16),
            V(rows, BF16),
            V(rows, F32),
            V((R_DEV, WIDE), BF16),
            V(rows, F32),
            V(rows, BF16),
            V((ROUNDS, EDGES, WIDE), BF16),
            V((EDGES, ROWS), BF16),
            V((EDGES, ROWS), BF16),
            V((ROWS, EDGES), BF16),
            V((ROWS, EDGES), BF16),
            V((EDGES, WIDE), BF16),
            V((EDGES, WIDE), BF16),
            V((EDGES, 1), F32),
            V((EDGES, NEG), BF16),
            V((2, EDGES, WIDE), BF16),
            V((2, EDGES, WIDE), BF16),
            V((NEG, WIDE), F32),
            V((NEG, WIDE), BF16),
            V(rows, F32),
            V(rows, BF16),
            V((4,) + rows, BF16),
            V((ROUNDS,) + rows, BF16),
            V(rows, BF16),
            V((R_DEV, WIDE), BF16),
            V((ROUNDS, R_DEV, WIDE), BF16),
            V((ROUNDS,) + panel, BF16),
            V((ROUNDS,) + panel, BF16),
            V((ROUNDS,) + panel, F32),
            V((ROUNDS,) + panel, F32),
            V((ROUNDS,) + half, F32),
            V((ROUNDS,) + half, F32),
            V((2 * ROUNDS,) + half, BF16),
            V((ROUNDS,) + half, BF16),
            V((ROUNDS,) + half, BF16),
            V((3,) + rows, BF16),
            V(rows, BF16),
            V((ROUNDS,) + rows, BF16),
            pltpu.SemaphoreType.DMA((7,)),
            pltpu.SemaphoreType.DMA((10,)),
            pltpu.SemaphoreType.DMA((10,)),
            pltpu.SemaphoreType.DMA((4, 8)),
            pltpu.SemaphoreType.DMA((4, 8)),
            pltpu.SemaphoreType.DMA((4, 4)),
            pltpu.SemaphoreType.DMA((4, 4)),
        ],
        compiler_params=pltpu.CompilerParams(
            collective_id=0, has_side_effects=True, vmem_limit_bytes=60 * 1024 * 1024
        ),
        name="train",
    )(
        offsets,
        counts.reshape(ROUNDS),
        embedding,
        adagrad.reshape(1, R_DEV),
        lhs_index,
        rhs_index,
        rel_ids,
        neg_index.reshape(ROUNDS, NEG),
        relation.T,
    )
    embedding_out, adagrad_out = pl.pallas_call(
        narrow,
        out_shape=[jax.ShapeDtypeStruct((R_DEV, D), F32), jax.ShapeDtypeStruct((1, R_DEV), F32)],
        in_specs=[vmem],
        out_specs=[vmem, vmem],
        name="narrow",
    )(state)
    return (embedding_out, adagrad_out.reshape(R_DEV))


def solution(mesh):
    return jax.shard_map(
        body,
        mesh=mesh,
        in_specs=(
            P(("dom", "row"), None),
            P(("dom", "row")),
            P(),
            P(),
            P(None, ("dom", "row")),
            P(None, ("dom", "row")),
            P(None, ("dom", "row")),
            P(None, ("dom", "row")),
            P(None, "dom", None),
        ),
        out_specs=(P(("dom", "row"), None), P(("dom", "row"))),
        check_vma=False,
    )
```

```python
import jax
import jax.numpy as jnp
from jax import lax
from jax.experimental import pallas as pl
from jax.experimental.pallas import tpu as pltpu
from jax.sharding import PartitionSpec as P

ROUNDS = 2
D = 400
HALF = 200
WIDE = 512
PART = 4
LANES = 128
SUM_PIECE, SUM_LANE = 1, 127
ND, NR, NX, NY, NZ = 64, 8, 4, 4, 16
R_DEV = 64
ROWS = 512
EDGES = 2048
NREL = 4096
NEG = 128
BLOCK = 256
BLOCKS = EDGES // BLOCK
STEP = 2048
STEPS = EDGES // STEP
LEARN = 0.1
MESH = pl.DeviceIdType.MESH
F32, BF16 = jnp.float32, jnp.bfloat16
NT = (((1,), (1,)), ((), ()))
TN = (((0,), (0,)), ((), ()))


def dot(a, b):
    return jnp.dot(a, b, preferred_element_type=F32)


def remote(src, dst, send, recv, device):
    return pltpu.make_async_remote_copy(
        src_ref=src, dst_ref=dst, send_sem=send, recv_sem=recv, device_id=device, device_id_type=MESH
    )


def panel_order(ids):
    owner = ids // R_DEV
    return (owner % 2) * (ROWS // 2) + (owner // 2) * R_DEV + ids % R_DEV


def as_column(row):
    return jnp.transpose(jnp.broadcast_to(row, (LANES, row.shape[1])))


def one_hot_rows(row, count):
    column = as_column(row)
    lane = lax.broadcasted_iota(jnp.int32, column.shape, 1)
    pieces = [(column == lane + first).astype(F32).astype(BF16) for first in range(0, count, LANES)]
    return jnp.concatenate(pieces, axis=1)


def one_hot_columns(row, count):
    place = lax.broadcasted_iota(jnp.int32, (count, row.shape[1]), 0)
    return (row == place).astype(F32).astype(BF16)


def split(value):
    high = value.astype(BF16)
    return high, (value - high.astype(F32)).astype(BF16)


def kernel(
    offsets, counts, embedding_in, adagrad_in, lhs_in, rhs_in, rel_in, neg_in, relation,
    out,
    embedding, adagrad, lhs, rhs, rel, neg, raw, work0, state0, head0, home, home_t, rel_rows, hot_h, hot_t, hot_ht, hot_tt, query, tail_rows, pos_weights, neg_weights, grad_h, grad_t, neg_sum, neg_rows,
    state, work, stage, tail_in, head_in, shard_h, shard_t, panel_h, panel_t,
    acc_h, acc_t, near_h, near_t, far_send, far_h, far_t, row_send, got_h, got_t,
    raw_sem, a2a_send, a2a_recv, ag_send, ag_recv, rs_send, rs_recv,
):
    me, row = lax.axis_index("dom"), lax.axis_index("row")
    x, core = row // 2, lax.rem(row, 2)
    y, z = me // NZ, lax.rem(me, NZ)
    sibling = x * 2 + 1 - core
    slot = core * NX + x

    barrier = pltpu.get_barrier_semaphore()

    def over_dom(act):
        def step(i, c):
            dz = NZ // 2 + (i + 1) // 2 * (1 - 2 * (i % 2))
            for dy in (2, 1, 3, 0):
                act(lax.rem(y + dy, NY) * NZ + lax.rem(z + dz, NZ))
            return c

        lax.fori_loop(0, NZ - 1, step, 0)
        for dy in (2, 1, 3):
            act(lax.rem(y + dy, NY) * NZ + z)

    over_dom(lambda t: pl.semaphore_signal(barrier, inc=1, device_id=(t, row), device_id_type=MESH))
    for j in range(1, NR):
        pl.semaphore_signal(barrier, inc=1, device_id=(me, lax.rem(row + j, NR)), device_id_type=MESH)

    fetches = [
        pltpu.make_async_copy(src, dst, raw_sem.at[number])
        for number, (src, dst) in enumerate(
            [
                (embedding_in, embedding),
                (adagrad_in, adagrad),
                (lhs_in, lhs),
                (rhs_in, rhs),
                (rel_in, rel),
                (neg_in, neg),
                (relation, raw),
            ]
        )
    ]
    for fetch in fetches:
        fetch.start()
    for fetch in fetches[:-1]:
        fetch.wait()

    gap = jnp.zeros((R_DEV, 256 - HALF), F32)
    wide = jnp.concatenate([embedding[:, :HALF], gap, embedding[:, HALF:], gap], axis=1)
    column = lax.broadcasted_iota(jnp.int32, (R_DEV, WIDE), 1)
    sums = as_column(jnp.concatenate([adagrad[...], adagrad[...]], axis=1))[:R_DEV, :1]
    state0[...] = jnp.where(column == SUM_PIECE * LANES + SUM_LANE, sums, wide).reshape(state0.shape)
    head0[...] = wide.astype(BF16)
    work0[...] = wide.reshape(work0.shape).astype(BF16)

    def relation_block(k, b):
        at = pl.ds(pl.multiple_of(b * BLOCK, BLOCK), BLOCK)
        found = dot(raw[...], one_hot_columns(rel[pl.ds(k, 1), at], NREL))
        hole = jnp.zeros((256 - HALF, BLOCK), F32)
        spaced = jnp.concatenate([found[:HALF], hole, found[HALF:], hole], axis=0)
        rel_rows[k, at, :] = jnp.transpose(spaced).astype(BF16)

    def relation_blocks(k, first, last):
        def step(b, c):
            relation_block(k, b)
            return c

        lax.fori_loop(first, last, step, 0)

    def selectors(k):
        def step(b, c):
            at = pl.ds(pl.multiple_of(b * BLOCK, BLOCK), BLOCK)
            head_ids = panel_order(lhs[pl.ds(k, 1), at])
            tail_ids = panel_order(rhs[pl.ds(k, 1), at])
            hot_h[at, :] = one_hot_rows(head_ids, ROWS)
            hot_t[at, :] = one_hot_rows(tail_ids, ROWS)
            hot_ht[:, at] = one_hot_columns(head_ids, ROWS)
            hot_tt[:, at] = one_hot_columns(tail_ids, ROWS)
            return c

        lax.fori_loop(0, BLOCKS, step, 0)

    def queries(k):
        panel = panel_h[k].reshape(ROWS, WIDE)

        def step(b, c):
            at = pl.ds(pl.multiple_of(b * STEP, STEP), STEP)
            heads = dot(hot_h[at, :], panel)
            rels = rel_rows[k, at, :].astype(F32)
            h_re, h_im = heads[:, :256], heads[:, 256:]
            c_re, c_im = rels[:, :256], rels[:, 256:]
            query[at, :256] = (h_re * c_re - h_im * c_im).astype(BF16)
            query[at, 256:] = (h_re * c_im + h_im * c_re).astype(BF16)
            return c

        lax.fori_loop(0, STEPS, step, 0)

    def tail_grads(k):
        panel = panel_t[k].reshape(ROWS, WIDE)
        neg_ids = panel_order(neg[pl.ds(k, 1), :])
        negatives = dot(one_hot_rows(neg_ids, ROWS), panel)
        neg_rows[...] = negatives.astype(BF16)
        neg_turned = jnp.transpose(negatives).astype(BF16)
        neg_sum[...] = jnp.zeros_like(neg_sum)
        count = counts[k]

        def step(b, c):
            at = pl.ds(pl.multiple_of(b * STEP, STEP), STEP)
            tails = dot(hot_t[at, :], panel)
            tail_rows[at, :] = tails.astype(BF16)
            q = query[at, :]
            q_f = q.astype(F32)
            positive = jnp.sum(q_f * tails, axis=1, keepdims=True)
            negative = dot(q, neg_turned)
            live = b * STEP + lax.broadcasted_iota(jnp.int32, (STEP, 1), 0) < count
            pos_weight = jnp.where(live, -1.0 / (1.0 + jnp.exp(positive)), 0.0)
            neg_weight = jnp.where(live, (1.0 / NEG) / (1.0 + jnp.exp(-negative)), 0.0).astype(BF16)
            pos_weights[at, :] = pos_weight
            neg_weights[at, :] = neg_weight
            high, low = split(pos_weight * q_f)
            grad_t[0, at, :] = high
            grad_t[1, at, :] = low
            neg_sum[...] += lax.dot_general(neg_weight, q, TN, preferred_element_type=F32)
            return c

        lax.fori_loop(0, STEPS, step, 0)

    def head_grads(k):
        def step(b, c):
            at = pl.ds(pl.multiple_of(b * STEP, STEP), STEP)
            g = pos_weights[at, :] * tail_rows[at, :].astype(F32) + dot(neg_weights[at, :], neg_rows[...])
            rels = rel_rows[k, at, :].astype(F32)
            g_re, g_im = g[:, :256], g[:, 256:]
            c_re, c_im = rels[:, :256], rels[:, 256:]
            high, low = split(g_re * c_re + g_im * c_im)
            grad_h[0, at, :256] = high
            grad_h[1, at, :256] = low
            high, low = split(g_im * c_re - g_re * c_im)
            grad_h[0, at, 256:] = high
            grad_h[1, at, 256:] = low
            return c

        lax.fori_loop(0, STEPS, step, 0)

    def tail_sums(k, half):
        rows = pl.ds(half * (ROWS // 2), ROWS // 2)
        hot_n = one_hot_columns(panel_order(neg[pl.ds(k, 1), :]) - half * (ROWS // 2), ROWS // 2)
        high, low = split(neg_sum[...])
        total = dot(hot_tt[rows, :], grad_t[0]) + dot(hot_tt[rows, :], grad_t[1]) + dot(hot_n, high) + dot(hot_n, low)
        acc_t[k, pl.ds(half * NX, NX)] = total.reshape(NX, R_DEV, WIDE)

    def head_sums(k, half):
        rows = pl.ds(half * (ROWS // 2), ROWS // 2)
        total = dot(hot_ht[rows, :], grad_h[0]) + dot(hot_ht[rows, :], grad_h[1])
        acc_h[k, pl.ds(half * NX, NX)] = total.reshape(NX, R_DEV, WIDE)

    def spread(number, src, dst):
        def send(t):
            remote(src.at[t], dst.at[me], a2a_send.at[number], a2a_recv.at[number], (t, row)).start()

        over_dom(send)
        dst[me] = src[me]

    def spread_all(number, src, dst):
        most = pl.ds(0, ND - 1)
        return remote(
            src.at[most], dst.at[most], a2a_send.at[number], a2a_recv.at[number], (lax.rem(me + 1, ND), row)
        )

    def spread_wait(number, src, dst):
        spread_all(number, src, dst).wait_recv()

    def rotated(k, src, dst, forward):
        by = offsets[k]
        shift = by if forward else ND - by

        def step(j, c):
            dst[j] = src[lax.rem(j + shift, ND)]
            return c

        lax.fori_loop(0, ND, step, 0, unroll=8)

    def gather_far(number, src, panel):
        copies = []
        for j in (2, 1, 3):
            t = lax.rem(x + j, NX) * 2 + core
            copies.append(remote(src, panel.at[slot], ag_send.at[number, j], ag_recv.at[number, j], (me, t)))
        return copies

    def gather_near(number, src, panel):
        return remote(src, panel.at[slot], ag_send.at[number, 0], ag_recv.at[number, 0], (me, sibling))

    def gather_start(number, src, panel):
        for copy in gather_far(number, src, panel):
            copy.start()
        gather_near(number, src, panel).start()
        panel[slot] = src[...]

    def gather_passed(number, panel):
        copies = []
        for j in (1, 3, 2):
            place = core * NX + lax.rem(x + NX - j, NX)
            copies.append(
                remote(
                    panel.at[place], panel.at[place], ag_send.at[number, NX + j], ag_recv.at[number, NX + j], (me, sibling)
                )
            )
        return copies

    def gather_pass(number, src, panel):
        opposite, right, left = gather_far(number, src, panel)
        for came, onward in zip((right, left, opposite), gather_passed(number, panel)):
            came.wait_recv()
            onward.start()

    def gather_end(number, src, panel):
        gather_near(number, src, panel).wait_recv()
        for copy in gather_passed(number, panel):
            copy.wait_recv()

    def gather_sent(number, src, panel):
        for copy in gather_far(number, src, panel) + [gather_near(number, src, panel)] + gather_passed(number, panel):
            copy.wait_send()

    def near_copy(number, acc, near):
        other = pl.ds((1 - core) * NX, NX)
        return remote(acc.at[other], near, rs_send.at[number, 0], rs_recv.at[number, 0], (me, sibling))

    def far_copies(number, far):
        copies = []
        for j in (2, 1, 3):
            t = lax.rem(x + j, NX)
            copies.append(
                remote(
                    far_send.at[number, t], far.at[j], rs_send.at[number, j], rs_recv.at[number, j], (me, t * 2 + core)
                )
            )
        return copies

    def sum_near(copy, number, acc, near, far):
        copy.wait_recv()
        near[...] = near[...] + acc[pl.ds(core * NX, NX)]
        far_send[number] = near[...].astype(BF16)
        for copy in far_copies(number, far):
            copy.start()

    def sum_far(number, near, far):
        for copy in far_copies(number, far):
            copy.wait_recv()
        return near[x] + (far[1].astype(F32) + far[2].astype(F32) + far[3].astype(F32))

    def is_sum():
        piece = lax.broadcasted_iota(jnp.int32, state.shape, 1)
        lane = lax.broadcasted_iota(jnp.int32, state.shape, 2)
        return (piece == SUM_PIECE) & (lane == SUM_LANE)

    def update(k):
        rotated(k, got_t.at[k], stage.at[2 + k], False)
        gradient = got_h[...].astype(F32) + stage[2 + k].astype(F32)
        at_sum = is_sum()
        now = state[...]
        squares = jnp.sum(jnp.where(at_sum, now, 0.0), axis=(1, 2), keepdims=True)
        squares = squares + jnp.sum(gradient * gradient, axis=(1, 2), keepdims=True) / D
        state[...] = jnp.where(at_sum, squares, now - LEARN * gradient / jnp.sqrt(squares))

    def finish(head_sum):
        gradient = head_sum + home_t[...].astype(F32).reshape(R_DEV, WIDE)
        now = home[...].reshape(R_DEV, WIDE)
        place = SUM_PIECE * LANES + SUM_LANE
        squares = now[:, place : place + 1] + jnp.sum(gradient * gradient, axis=1, keepdims=True) / D
        now = now - LEARN * gradient / jnp.sqrt(squares)
        column = lax.broadcasted_iota(jnp.int32, now.shape, 1)
        out[...] = jnp.where(column == place, squares, now)

    def to_rows(value):
        return value.reshape(R_DEV, PART, LANES).astype(BF16)

    def to_shard(value):
        return value.astype(F32).reshape(R_DEV, WIDE).astype(BF16)

    selectors(0)
    fetches[-1].wait()
    relation_blocks(0, 0, 2)

    pl.semaphore_wait(barrier, ND - 1 + NR - 1)
    spread(0, work0, work)
    gather_start(0, head0, panel_h.at[0])
    relation_blocks(0, 2, 6)
    gather_pass(0, head0, panel_h.at[0])
    spread_wait(0, work0, work)
    rotated(0, work, stage.at[0], True)
    spread(1, stage.at[0], tail_in.at[0])
    relation_blocks(0, 6, 8)
    gather_end(0, head0, panel_h.at[0])
    queries(0)
    spread_wait(1, stage.at[0], tail_in.at[0])
    shard_t[0] = to_shard(tail_in[0])
    gather_start(1, shard_t.at[0], panel_t.at[0])
    spread(9, state0, state)
    relation_blocks(1, 0, 2)
    gather_pass(1, shard_t.at[0], panel_t.at[0])
    relation_blocks(1, 2, 3)
    gather_end(1, shard_t.at[0], panel_t.at[0])

    for k in range(ROUNDS):
        last = k == ROUNDS - 1
        if k > 0:
            spread_wait(4, work, head_in)
            shard_h[...] = to_shard(head_in[...])
            gather_start(2, shard_h, panel_h.at[1])
            spread_wait(5, stage.at[1], tail_in.at[1])
            shard_t[1] = to_shard(tail_in[1])
            gather_start(3, shard_t.at[1], panel_t.at[1])
            spread(7, state, home)
            gather_pass(2, shard_h, panel_h.at[1])
            gather_pass(3, shard_t.at[1], panel_t.at[1])
            gather_end(2, shard_h, panel_h.at[1])
            queries(1)
            gather_end(3, shard_t.at[1], panel_t.at[1])
        near_tail, near_head = (near_copy(2 * k, acc_t.at[k], near_t.at[k]), near_copy(2 * k + 1, acc_h.at[k], near_h.at[k]))
        tail_grads(k)
        if not last:
            head_grads(k)
            tail_sums(k, 1 - core)
            near_tail.start()
            head_sums(k, 1 - core)
            near_head.start()
            tail_sums(k, core)
            sum_near(near_tail, 2 * k, acc_t.at[k], near_t.at[k], far_t.at[k])
            head_sums(k, core)
            sum_near(near_head, 2 * k + 1, acc_h.at[k], near_h.at[k], far_h.at[k])
            relation_blocks(1, 3, 5)
            row_send[0] = to_rows(sum_far(0, near_t.at[0], far_t.at[0]))
            spread(2, row_send.at[0], got_t.at[0])
            row_send[1] = to_rows(sum_far(1, near_h.at[0], far_h.at[0]))
            spread(3, row_send.at[1], got_h)
            relation_blocks(1, 5, 8)
            selectors(1)
            spread_wait(9, state0, state)
            spread_wait(2, row_send.at[0], got_t.at[0])
            spread_wait(3, row_send.at[1], got_h)
            update(0)
            work[...] = jnp.where(is_sum(), 0.0, state[...]).astype(BF16)
            spread(4, work, head_in)
            rotated(1, work, stage.at[1], True)
            spread(5, stage.at[1], tail_in.at[1])
        else:
            tail_sums(k, 1 - core)
            near_tail.start()
            tail_sums(k, core)
            sum_near(near_tail, 2 * k, acc_t.at[k], near_t.at[k], far_t.at[k])
            head_grads(k)
            head_sums(k, 1 - core)
            head_sums(k, core)
            row_send[2] = to_rows(sum_far(2, near_t.at[1], far_t.at[1]))
            spread(6, row_send.at[2], got_t.at[1])
            near_head.start()
            sum_near(near_head, 2 * k + 1, acc_h.at[k], near_h.at[k], far_h.at[k])
            head_sum = sum_far(2 * k + 1, near_h.at[k], far_h.at[k])
            spread_wait(7, state, home)
            spread_wait(6, row_send.at[2], got_t.at[1])
            rotated(1, got_t.at[1], stage.at[3], False)
            spread(8, stage.at[3], home_t)
            spread_wait(8, stage.at[3], home_t)
            finish(head_sum)

    for number, src, dst in (
        (0, work0, work),
        (1, stage.at[0], tail_in.at[0]),
        (2, row_send.at[0], got_t.at[0]),
        (3, row_send.at[1], got_h),
        (4, work, head_in),
        (5, stage.at[1], tail_in.at[1]),
        (6, row_send.at[2], got_t.at[1]),
        (7, state, home),
        (8, stage.at[3], home_t),
        (9, state0, state),
    ):
        spread_all(number, src, dst).wait_send()
    gather_sent(0, head0, panel_h.at[0])
    gather_sent(1, shard_t.at[0], panel_t.at[0])
    gather_sent(2, shard_h, panel_h.at[1])
    gather_sent(3, shard_t.at[1], panel_t.at[1])
    for k in range(ROUNDS):
        for number, acc, near, far in ((2 * k, acc_t, near_t, far_t), (2 * k + 1, acc_h, near_h, far_h)):
            near_copy(number, acc.at[k], near.at[k]).wait_send()
            for copy in far_copies(number, far.at[k]):
                copy.wait_send()


def narrow(state, embedding_out, adagrad_out):
    now = state[...]
    embedding_out[...] = jnp.concatenate([now[:, :HALF], now[:, 256 : 256 + HALF]], axis=1)
    place = SUM_PIECE * LANES + SUM_LANE
    squares = jnp.broadcast_to(now[:, place : place + 1], (R_DEV, LANES))
    adagrad_out[...] = jnp.transpose(jnp.concatenate([squares, squares], axis=0))[:1, :R_DEV]


def body(embedding, adagrad, relation, offsets, counts, lhs_index, rhs_index, rel_ids, neg_index):
    vmem = pl.BlockSpec(memory_space=pltpu.VMEM)
    smem = pl.BlockSpec(memory_space=pltpu.SMEM)
    rows = (R_DEV, PART, LANES)
    panel = (NR, R_DEV, WIDE)
    half = (NX, R_DEV, WIDE)
    V = pltpu.VMEM
    state = pl.pallas_call(
        kernel,
        out_shape=jax.ShapeDtypeStruct((R_DEV, WIDE), F32),
        in_specs=[smem, smem] + [pl.BlockSpec(memory_space=pl.ANY)] * 7,
        out_specs=vmem,
        scratch_shapes=[
            V((R_DEV, D), F32),
            V((1, R_DEV), F32),
            V((ROUNDS, EDGES), jnp.int32),
            V((ROUNDS, EDGES), jnp.int32),
            V((ROUNDS, EDGES), jnp.int32),
            V((ROUNDS, NEG), jnp.int32),
            V((D, NREL), BF16),
            V(rows, BF16),
            V(rows, F32),
            V((R_DEV, WIDE), BF16),
            V(rows, F32),
            V(rows, BF16),
            V((ROUNDS, EDGES, WIDE), BF16),
            V((EDGES, ROWS), BF16),
            V((EDGES, ROWS), BF16),
            V((ROWS, EDGES), BF16),
            V((ROWS, EDGES), BF16),
            V((EDGES, WIDE), BF16),
            V((EDGES, WIDE), BF16),
            V((EDGES, 1), F32),
            V((EDGES, NEG), BF16),
            V((2, EDGES, WIDE), BF16),
            V((2, EDGES, WIDE), BF16),
            V((NEG, WIDE), F32),
            V((NEG, WIDE), BF16),
            V(rows, F32),
            V(rows, BF16),
            V((4,) + rows, BF16),
            V((ROUNDS,) + rows, BF16),
            V(rows, BF16),
            V((R_DEV, WIDE), BF16),
            V((ROUNDS, R_DEV, WIDE), BF16),
            V((ROUNDS,) + panel, BF16),
            V((ROUNDS,) + panel, BF16),
            V((ROUNDS,) + panel, F32),
            V((ROUNDS,) + panel, F32),
            V((ROUNDS,) + half, F32),
            V((ROUNDS,) + half, F32),
            V((2 * ROUNDS,) + half, BF16),
            V((ROUNDS,) + half, BF16),
            V((ROUNDS,) + half, BF16),
            V((3,) + rows, BF16),
            V(rows, BF16),
            V((ROUNDS,) + rows, BF16),
            pltpu.SemaphoreType.DMA((7,)),
            pltpu.SemaphoreType.DMA((10,)),
            pltpu.SemaphoreType.DMA((10,)),
            pltpu.SemaphoreType.DMA((4, 8)),
            pltpu.SemaphoreType.DMA((4, 8)),
            pltpu.SemaphoreType.DMA((4, 4)),
            pltpu.SemaphoreType.DMA((4, 4)),
        ],
        compiler_params=pltpu.CompilerParams(
            collective_id=0, has_side_effects=True, vmem_limit_bytes=60 * 1024 * 1024
        ),
        name="train",
    )(
        offsets,
        counts.reshape(ROUNDS),
        embedding,
        adagrad.reshape(1, R_DEV),
        lhs_index,
        rhs_index,
        rel_ids,
        neg_index.reshape(ROUNDS, NEG),
        relation.T,
    )
    embedding_out, adagrad_out = pl.pallas_call(
        narrow,
        out_shape=[jax.ShapeDtypeStruct((R_DEV, D), F32), jax.ShapeDtypeStruct((1, R_DEV), F32)],
        in_specs=[vmem],
        out_specs=[vmem, vmem],
        name="narrow",
    )(state)
    return (embedding_out, adagrad_out.reshape(R_DEV))


def solution(mesh):
    return jax.shard_map(
        body,
        mesh=mesh,
        in_specs=(
            P(("dom", "row"), None),
            P(("dom", "row")),
            P(),
            P(),
            P(None, ("dom", "row")),
            P(None, ("dom", "row")),
            P(None, ("dom", "row")),
            P(None, ("dom", "row")),
            P(None, "dom", None),
        ),
        out_specs=(P(("dom", "row"), None), P(("dom", "row"))),
        check_vma=False,
    )
```
